32 devices in a mesh: parts: 2 (over x), role: 2 (over core), shard: 8 (over z, y).
Axes of the slice: x: 2, y: 2, z: 4, core: 2. Of those that a mesh axis runs over, the one named last changes fastest.
Arguments:
- states: bfloat16 [4096, 7168], P(('parts', 'shard')), parts along dimension 0, may hold values from -6 to 6
- w_latent: bfloat16 [7168, 512], P('role'), may hold values from -0.0625 to 0.0625
- w_rope: bfloat16 [7168, 64], P('role'), may hold values from -0.0625 to 0.0625
- latent_gain: bfloat16 [512], replicated, may hold values from 0.25 to 1.75
- span_len: int32 [16, 4], P('parts'), parts along dimension 0, may hold values from 1 to 128, 256 in all within a row
- cache_len: int32 [16, 4], P('parts'), parts along dimension 0, may hold values from 1 to 256
- dest: int32 [16, 4], P('parts'), parts along dimension 0, may hold values from 0 to 7, all different within a row; in each aligned block of 8 rows (0 to 7, 8 to 15, ...) at most 8 rows name the same one
- page_table: int32 [16, 24], P(('parts', 'shard')), parts along dimension 0, may hold values from 0 to 23, each once within a row
- latent_pool: bfloat16 [384, 128, 512], P(('parts', 'shard')), parts along dimension 0, may hold values from -6 to 6
- rope_pool: bfloat16 [384, 64, 128], P(('parts', 'shard')), parts along dimension 0, may hold values from -6 to 6
- new_keys: bfloat16 [16, 8, 4, 576], P(('parts', 'shard')), parts along dimension 0, may hold values from -6 to 6
- q_nope: bfloat16 [4, 64, 16384], P(None, 'parts', 'shard'), parts along dimension 1, may hold values from -6 to 6
- q_rope: bfloat16 [4, 64, 8192], P(None, 'parts', 'shard'), parts along dimension 1, may hold values from -64 to 64
- w_uk: bfloat16 [128, 128, 512], P('shard'), may hold values from -0.5 to 0.5
- w_uv: bfloat16 [128, 512, 128], P('shard'), may hold values from -0.25 to 0.25
Outputs:
- head_outputs: bfloat16 [64, 4, 16384], P(('parts', 'role'), None, 'shard'), parts along dimension 0
The draws below stay inside these ranges and needn't reach their ends.
There are 2 independent parts, one for each index of `parts`. The reference program is written for one: setup_inputs(seed, part) draws one part's arguments, and reference() takes and returns one part's arrays. A program takes and returns all parts, laid end to end along the dimension named above; an argument that names none is the same for every part. Nothing has to cross between parts.
Inputs may be any that keep to these rules, and one draw needn't show every extreme that they name: `dest`: A prefill rank's 4 requests go to distinct decode ranks; at most 8 requests of a group go to one decode rank, and some rank receives exactly 8; every rank receives at least one. `span_len`: the 4 lengths of a prefill rank sum to 256; the largest of each rank is 128. `page_table`: each row is a permutation of 0 to 23.
All inputs are finite; a program needn't handle non-finite values.
Results may differ from the reference program's by a relative error of at most 0.0074.
Values may be sent and summed in bfloat16 or wider, within the bound.
A program may use at most 128 MiB of HBM per device.

```python
import math
import jax
import jax.numpy as jnp
import numpy as np
from jax import lax

D = 7168
LAT = 512
ROPE = 64
H = 128
HD = 128
VD = 128
PAGE = 128
STEPS = 4
PREQ = 4
REQ_CAP = 8
PTOK = 256
PMAX = 128
CMAX = 256
PAGES_REQ = 3
POOL_DEV = 24
KROWS = 384
NREQ = 32
N_SHARD = 8


def draw_q_rope(key, part):
    key = jax.random.fold_in(key, 17)
    background_key = jax.random.fold_in(key, 0)
    values = jnp.clip(jax.random.normal(background_key, (STEPS, NREQ, H, ROPE), jnp.float32), -6.0, 6.0)
    return values.reshape(STEPS, NREQ, H * ROPE).astype(jnp.bfloat16)


def draw_new_keys(key, part):
    key = jax.random.fold_in(key, 29)
    latent_key = jax.random.fold_in(key, 0)
    values = jnp.clip(jax.random.normal(latent_key, (N_SHARD, REQ_CAP, STEPS, LAT + ROPE), jnp.float32), -6.0, 6.0)
    return values.astype(jnp.bfloat16)


def touch_ends(result, stream_key, smallest, high):
    longest = result.shape.index(max(result.shape))
    spots = []
    for shift in (0, 1):
        where = [jax.random.randint(jax.random.fold_in(stream_key, axis), (), 0, length) for axis, length in enumerate(result.shape)]
        where[longest] = (where[longest] + shift) % result.shape[longest]
        spots.append(tuple(where))
    return result.at[spots[0]].set(smallest).at[spots[1]].set(high)


def level_of(key, extent, cuts, least, largest):
    def one(dim, shards_of):
        steps = jax.random.uniform(jax.random.fold_in(jax.random.fold_in(key, 6), dim), (shards_of,), jnp.float32, least / len(cuts), largest / len(cuts))
        return jnp.repeat(jnp.exp(steps), extent[dim] // shards_of).reshape((-1,) + (1,) * (len(extent) - dim - 1))

    gain = one(*cuts[0])
    for cut in cuts[1:]:
        gain = gain * one(*cut)
    return gain


def profile(count, total, limit, lean):
    loads = [(1 << 20) // math.isqrt(standing ** lean) + 1 for standing in range(2, count + 1)]
    surplus, given = total - limit - (count - 1), [1] * (count - 1)
    while surplus > 0:
        movable = [i for i in range(count - 1) if given[i] < limit]
        pool, remaining = sum([loads[i] for i in movable]), surplus
        for i in movable:
            extra = min(limit - given[i], max(1, remaining * loads[i] // pool), surplus)
            given[i] = given[i] + extra
            surplus = surplus - extra
    return np.array([limit] + given)


def uneven(own_key, number_of, total, most, slope):
    if number_of == 2:
        one = jax.random.randint(own_key, (), max(1, total - most), min(most, total - 1) + 1)
        return jnp.stack([one, total - one])
    lengths = jnp.asarray(profile(number_of, total, most, slope), jnp.int32)
    twos = (number_of - 1) // 2
    donor, sink = lengths[1:1 + 2 * twos:2], lengths[2:2 + 2 * twos:2]
    room = jnp.minimum(donor - 1, most - sink)
    moved = jax.random.randint(jax.random.fold_in(own_key, 1), (twos,), 0, 1 << 20) % (room + 1)
    lengths = lengths.at[1:1 + 2 * twos:2].set(donor - moved).at[2:2 + 2 * twos:2].set(sink + moved)
    return lengths[jax.random.permutation(jax.random.fold_in(own_key, 2), number_of)]


def routed_block(stream_key, own, number, rows, amount, top, bound, lean):
    order = jax.random.permutation(stream_key, amount)
    crowded, usual = load_shares(amount, rows * top, bound, lean, True), load_shares(amount, rows * top, bound, lean, False)
    places = jnp.arange(amount)

    def named(sizes, rotation):
        used = int((sizes > 0).sum())
        fixed = max(1, used // 4)
        moved = fixed + (places - fixed + rotation * (used - fixed)) % max(1, amount - fixed)
        return jnp.zeros((amount,), jnp.int32).at[order[jnp.where(places < fixed, places, moved)]].set(jnp.asarray(sizes, jnp.int32))

    sizes = jnp.where(number % 4 == 0, named(crowded, number // 4), named(usual, number - number // 4 - 1))
    mixed = jax.random.permutation(jax.random.fold_in(own, 3), amount)
    giver, receiver = mixed[0:amount // 2 * 2:2], mixed[1:amount // 2 * 2:2]
    margin = jnp.minimum(sizes[giver] - 1, bound - sizes[receiver]) // 2
    margin = jnp.where((giver == order[0]) | (receiver == order[0]) | (sizes[receiver] == 0), 0, jnp.maximum(margin, 0))
    moved = jax.random.randint(jax.random.fold_in(own, 4), (amount // 2,), 0, 1 << 20) % (margin + 1)
    sizes = sizes.at[giver].add(-moved).at[receiver].add(moved)
    members = jnp.searchsorted(jnp.cumsum(sizes), jnp.arange(rows * top), side="right").astype(jnp.int32)
    listing = members.reshape(top, rows).T
    listing = listing[jax.random.permutation(jax.random.fold_in(own, 1), rows)]
    rotation = jax.random.randint(jax.random.fold_in(own, 2), (rows, 1), 0, top)
    return jnp.take_along_axis(listing, (jnp.arange(top)[None, :] + rotation) % top, axis=1)


def load_shares(number_of, total, reach, slope, full):
    weights = [(1 << 20) // math.isqrt(grade ** slope) + 1 for grade in range(1, number_of + 1)]
    largest = reach if full else min(reach, max(-(-total // number_of), total * weights[0] // sum(weights)))
    least = 1 if total - largest >= number_of - 1 else 0
    holding, surplus = [largest] + [least] * (number_of - 1), total - largest - least * (number_of - 1)
    while surplus > 0:
        movable = [i for i in range(1, number_of) if holding[i] < largest] or [i for i in range(1, number_of) if holding[i] < reach]
        whole, remaining = sum([weights[i] for i in movable]), surplus
        for i in movable:
            extra = min(reach - holding[i], max(1, remaining * weights[i] // whole), surplus)
            holding[i] = holding[i] + extra
            surplus = surplus - extra
    return np.array(holding)


def bell_draw(rng, extent, scale, reach, pieces=(), kind=jnp.bfloat16):
    factor_of = level_of(rng, extent, pieces, -0.22, 0.18) if pieces else 1.0
    values = jax.random.normal(rng, extent, jnp.float32) * scale * factor_of
    return jnp.minimum(jnp.maximum(values, -reach), reach).astype(kind)


def setup_inputs(seed: int = 0, part: int = 0) -> dict:
    keys = jax.random.split(jax.random.key(seed), 16)
    part_splits = jax.random.split(jax.random.fold_in(keys[15], part), 16)
    states = bell_draw(part_splits[0], (N_SHARD * PTOK, D), 1.0, 6.0, ((0, 8),))
    w_latent = bell_draw(keys[1], (D, LAT), D ** -0.5, 0.0625, ((0, 2),))
    w_rope = bell_draw(keys[2], (D, ROPE), D ** -0.5, 0.0625, ((0, 2),))
    latent_gain = jnp.clip(1.0 + 0.15 * jax.random.normal(keys[3], (LAT,), jnp.float32), 0.25, 1.75).astype(jnp.bfloat16)
    span_len = jax.vmap(lambda own: uneven(own, PREQ, PTOK, PMAX, 2))(jax.random.split(part_splits[4], N_SHARD)).reshape((N_SHARD, PREQ)).astype(jnp.int32)
    cache_len = touch_ends(jax.random.randint(part_splits[5], (N_SHARD, PREQ), 1, CMAX + 1), jax.random.fold_in(part_splits[5], 1), 1, CMAX).astype(jnp.int32)
    dest_keys = jax.random.split(jax.random.fold_in(part_splits[6], 1), N_SHARD // N_SHARD)
    dest_turns = jax.random.permutation(jax.random.fold_in(part_splits[6], 3), N_SHARD // N_SHARD)
    dest = jax.vmap(lambda own, number: routed_block(jax.random.fold_in(part_splits[6], 2), own, number, N_SHARD, N_SHARD, PREQ, REQ_CAP, 2))(dest_keys, dest_turns).reshape((N_SHARD, PREQ))
    page_table = jax.vmap(lambda own: jax.random.permutation(own, POOL_DEV))(jax.random.split(part_splits[7], N_SHARD)).reshape((N_SHARD, POOL_DEV)).astype(jnp.int32)
    latent_pool = bell_draw(part_splits[8], (N_SHARD * POOL_DEV, PAGE, LAT), 1.0, 6.0, ((0, 8),))
    rope_pool = bell_draw(part_splits[9], (N_SHARD * POOL_DEV, ROPE, PAGE), 1.0, 6.0, ((0, 8),))
    new_keys = draw_new_keys(jax.random.fold_in(jax.random.fold_in(keys[15], part), 71), part)
    q_nope = bell_draw(part_splits[11], (STEPS, NREQ, H * HD), 1.0, 6.0, ((2, 8),))
    q_rope = draw_q_rope(jax.random.fold_in(jax.random.fold_in(keys[15], part), 71), part)
    w_uk = bell_draw(keys[13], (H, HD, LAT), HD ** -0.5, 0.5, ((0, 8),))
    w_uv = bell_draw(keys[14], (H, LAT, VD), LAT ** -0.5, 0.25, ((0, 8),))
    return dict(states=states, w_latent=w_latent, w_rope=w_rope, latent_gain=latent_gain, span_len=span_len, cache_len=cache_len, dest=dest, page_table=page_table, latent_pool=latent_pool, rope_pool=rope_pool, new_keys=new_keys, q_nope=q_nope, q_rope=q_rope, w_uk=w_uk, w_uv=w_uv)


def rotate_rows(values, positions):
    half_width = values.shape[-1] // 2
    frequency = 10000.0 ** (-jnp.arange(half_width, dtype=jnp.float32) / half_width)
    angles = positions.astype(jnp.float32)[:, None] * frequency[None, :]
    cosine = jnp.cos(angles)
    sine = jnp.sin(angles)
    first_half = values[:, :half_width]
    second_half = values[:, half_width:]
    return jnp.concatenate([first_half * cosine - second_half * sine, first_half * sine + second_half * cosine], axis=1)

def span_positions(span_rows, cached_rows, row_count):
    segment_end = jnp.cumsum(span_rows).astype(jnp.int32)
    starts = (segment_end - span_rows).astype(jnp.int32)
    row_ids = jnp.arange(row_count, dtype=jnp.int32)
    segment = lax.optimization_barrier(jnp.sum((row_ids[:, None] >= segment_end[None, :]).astype(jnp.int32), axis=1)).astype(jnp.int32)
    member = segment[:, None] == jnp.arange(span_rows.shape[0], dtype=jnp.int32)[None, :]
    shifted = lax.optimization_barrier(jnp.sum(jnp.where(member, (cached_rows - starts)[None, :], 0), axis=1)).astype(jnp.int32)
    return row_ids + shifted

def reference(states, w_latent, w_rope, latent_gain, span_len, cache_len, dest, page_table, latent_pool, rope_pool, new_keys, q_nope, q_rope, w_uk, w_uv):
    latent_raw = jnp.dot(states, w_latent, preferred_element_type=jnp.float32)
    mean_square = lax.optimization_barrier(jnp.mean(latent_raw * latent_raw, axis=1, keepdims=True))
    latent_rows = (latent_raw * lax.rsqrt(mean_square + 1e-06) * latent_gain.astype(jnp.float32)).astype(jnp.bfloat16)
    latent_rows = latent_rows.reshape(N_SHARD, PTOK, LAT)
    rope_raw = jnp.dot(states, w_rope, preferred_element_type=jnp.float32).reshape(N_SHARD, PTOK, ROPE)
    positions = jax.vmap(lambda span_rows, cached_rows: span_positions(span_rows, cached_rows, PTOK))(span_len, cache_len)
    rope_rows = jax.vmap(rotate_rows)(rope_raw, positions).astype(jnp.bfloat16)
    dest_flat = dest.reshape(-1)
    rank_hit = (dest_flat[:, None] == jnp.arange(N_SHARD, dtype=jnp.int32)[None, :]).astype(jnp.int32)
    slot_of = lax.optimization_barrier(jnp.sum((jnp.cumsum(rank_hit, axis=0) - rank_hit) * rank_hit, axis=1)).astype(jnp.int32)
    starts = (jnp.cumsum(span_len, axis=1) - span_len).reshape(-1).astype(jnp.int32)
    cached_flat = cache_len.reshape(-1).astype(jnp.int32)
    total_flat = (cache_len + span_len).reshape(-1).astype(jnp.int32)
    source_flat = jnp.arange(NREQ, dtype=jnp.int32) // PREQ
    uk_wide = w_uk.astype(jnp.float32)
    uv_wide = w_uv.astype(jnp.float32)
    nope_rows = jnp.swapaxes(q_nope, 0, 1)
    rope_query_rows = jnp.swapaxes(q_rope, 0, 1)
    score_scale = (HD + ROPE) ** (-0.5)
    key_position = jnp.arange(KROWS, dtype=jnp.int32)
    causal = jnp.arange(STEPS)[None, :] <= jnp.arange(STEPS)[:, None]

    def one_request(request_item):
        decode_rank, slot_index, source, span_start, cached, row_total, nope_query, rope_query = request_item
        entries = lax.dynamic_slice(page_table, (decode_rank, slot_index * PAGES_REQ), (1, PAGES_REQ))[0] + decode_rank * POOL_DEV
        pool_latent = latent_pool[entries].reshape(KROWS, LAT)
        pool_rope = jnp.swapaxes(rope_pool[entries], 1, 2).reshape(KROWS, ROPE)
        from_span = (key_position >= cached) & (key_position < row_total)
        span_index = jnp.clip(span_start + key_position - cached, 0, PTOK - 1)
        key_latent = jnp.where(from_span[:, None], latent_rows[source][span_index], pool_latent).astype(jnp.float32)
        key_rope = jnp.where(from_span[:, None], rope_rows[source][span_index], pool_rope).astype(jnp.float32)
        recent = new_keys[decode_rank, slot_index].astype(jnp.float32)
        recent_latent = recent[:, :LAT]
        recent_rope = recent[:, LAT:]
        query_latent = jnp.einsum('thd,hdl->thl', nope_query.reshape(STEPS, H, HD).astype(jnp.float32), uk_wide)
        query_latent = query_latent.astype(jnp.bfloat16).astype(jnp.float32)
        query_rope = rope_query.reshape(STEPS, H, ROPE).astype(jnp.float32)
        cache_score = (jnp.einsum('thl,pl->thp', query_latent, key_latent) + jnp.einsum('the,pe->thp', query_rope, key_rope)) * score_scale
        recent_score = (jnp.einsum('thl,ul->thu', query_latent, recent_latent) + jnp.einsum('the,ue->thu', query_rope, recent_rope)) * score_scale
        live_mask = (key_position < row_total)[None, None, :]
        causal_mask = causal[:, None, :]
        cache_score = jnp.where(live_mask, cache_score, -1e+30)
        recent_score = jnp.where(causal_mask, recent_score, -1e+30)
        row_peak = jnp.maximum(lax.optimization_barrier(jnp.max(cache_score, axis=-1)), lax.optimization_barrier(jnp.max(recent_score, axis=-1)))[..., None]
        cache_weight = jnp.where(live_mask, jnp.exp(cache_score - row_peak), 0.0)
        recent_weight = jnp.where(causal_mask, jnp.exp(recent_score - row_peak), 0.0)
        norm_total = lax.optimization_barrier(jnp.sum(cache_weight, axis=-1)) + lax.optimization_barrier(jnp.sum(recent_weight, axis=-1))
        cache_low = cache_weight.astype(jnp.bfloat16).astype(jnp.float32)
        recent_low = recent_weight.astype(jnp.bfloat16).astype(jnp.float32)
        weighted = jnp.einsum('thp,pl->thl', cache_low, key_latent) + jnp.einsum('thu,ul->thl', recent_low, recent_latent)
        attended = (weighted / norm_total[..., None]).astype(jnp.bfloat16).astype(jnp.float32)
        projected = jnp.einsum('thl,hlv->thv', attended, uv_wide)
        return projected.astype(jnp.bfloat16).reshape(STEPS, H * VD)
    return lax.map(one_request, (dest_flat, slot_of, source_flat, starts, cached_flat, total_flat, nope_rows, rope_query_rows))
```

```python
import functools

import jax
import jax.numpy as jnp
from jax import lax
from jax.experimental import pallas as pl
from jax.experimental.pallas import tpu as pltpu
from jax.sharding import PartitionSpec as P

MESH = pl.DeviceIdType.MESH


def rotate_rows(values, positions):
    half_width = values.shape[-1] // 2
    frequency = 10000.0 ** (-jnp.arange(half_width, dtype=jnp.float32) / half_width)
    angles = positions.astype(jnp.float32)[:, None] * frequency[None, :]
    cosine = jnp.cos(angles)
    sine = jnp.sin(angles)
    first_half = values[:, :half_width]
    second_half = values[:, half_width:]
    return jnp.concatenate(
        [first_half * cosine - second_half * sine, first_half * sine + second_half * cosine], axis=1
    )


def span_positions(span_rows, cached_rows, row_count):
    segment_end = jnp.cumsum(span_rows)
    starts = segment_end - span_rows
    row_ids = jnp.arange(row_count, dtype=jnp.int32)
    segment = jnp.sum((row_ids[:, None] >= segment_end[None, :]).astype(jnp.int32), axis=1)
    member = segment[:, None] == jnp.arange(span_rows.shape[0], dtype=jnp.int32)[None, :]
    shifted = jnp.sum(jnp.where(member, (cached_rows - starts)[None, :], 0), axis=1)
    return row_ids + shifted


def exchange_kernel(count, shards, *refs):
    sources, targets = refs[:count], refs[count : 2 * count]
    send_sem, recv_sem, local_sem = refs[2 * count :]
    me = lax.axis_index("shard")
    barrier = pltpu.get_barrier_semaphore()
    for step in range(1, shards):
        peer = lax.rem(me + step, shards)
        pl.semaphore_signal(barrier, inc=1, device_id={"shard": peer}, device_id_type=MESH)
    pl.semaphore_wait(barrier, shards - 1)

    def remote(index, step):
        peer = lax.rem(me + step, shards)
        return pltpu.make_async_remote_copy(
            src_ref=sources[index].at[peer],
            dst_ref=targets[index].at[me],
            send_sem=send_sem.at[index, step],
            recv_sem=recv_sem.at[index, step],
            device_id={"shard": peer},
            device_id_type=MESH,
        )

    def arriving(index, step):
        origin = lax.rem(me + shards - step, shards)
        return pltpu.make_async_remote_copy(
            src_ref=sources[index].at[me],
            dst_ref=targets[index].at[origin],
            send_sem=send_sem.at[index, step],
            recv_sem=recv_sem.at[index, step],
            device_id={"shard": origin},
            device_id_type=MESH,
        )

    for index in range(count):
        for step in range(1, shards):
            remote(index, step).start()
    local = [
        pltpu.make_async_copy(sources[i].at[me], targets[i].at[me], local_sem.at[i])
        for i in range(count)
    ]
    for copy in local:
        copy.start()
    for copy in local:
        copy.wait()
    for index in range(count):
        for step in range(1, shards):
            arriving(index, step).wait_recv()
            remote(index, step).wait_send()


def exchange(arrays, shards, collective_id):
    count = len(arrays)
    return pl.pallas_call(
        functools.partial(exchange_kernel, count, shards),
        out_shape=[jax.ShapeDtypeStruct(a.shape, a.dtype) for a in arrays],
        in_specs=[pl.BlockSpec(memory_space=pl.ANY)] * count,
        out_specs=[pl.BlockSpec(memory_space=pl.ANY)] * count,
        scratch_shapes=[
            pltpu.SemaphoreType.DMA((count, shards)),
            pltpu.SemaphoreType.DMA((count, shards)),
            pltpu.SemaphoreType.DMA((count,)),
        ],
        compiler_params=pltpu.CompilerParams(collective_id=collective_id, has_side_effects=True),
    )(*arrays)


def attention_kernel(
    scale,
    heads,
    page_rows,
    steps,
    info_ref,
    ql_ref,
    qr_ref,
    mine_latent,
    mine_rope,
    other_latent,
    other_rope,
    span_latent,
    span_rope,
    new_latent,
    new_rope,
    out_ref,
):
    j = pl.program_id(0)
    role = info_ref[0]
    cached = info_ref[1 + 3 * j]
    start = info_ref[2 + 3 * j]
    length = info_ref[3 + 3 * j]
    shards, each, width = ql_ref.shape
    rows = shards * each
    ql = ql_ref[...].reshape(rows, width)
    qr = qr_ref[0]
    contract_last = (((1,), (1,)), ((), ()))

    def dot_last(a, b):
        return lax.dot_general(a, b, contract_last, preferred_element_type=jnp.float32)

    def dot(a, b):
        return jnp.dot(a, b, preferred_element_type=jnp.float32)

    def column(n):
        return lax.broadcasted_iota(jnp.int32, (rows, n), 1)

    low = -1e30
    score_mine = (dot_last(ql, mine_latent[0]) + dot(qr, mine_rope[0])) * scale
    live_mine = column(page_rows) + role * page_rows < cached
    score_mine = jnp.where(live_mine, score_mine, low)
    score_other = (dot_last(ql, other_latent[0]) + dot(qr, other_rope[0])) * scale
    live_other = column(page_rows) + (1 - role) * page_rows < cached
    score_other = jnp.where(live_other, score_other, low)
    score_span = (dot_last(ql, span_latent[...]) + dot_last(qr, span_rope[...])) * scale
    span_col = column(span_latent.shape[0])
    live_span = (span_col >= start) & (span_col < start + length)
    score_span = jnp.where(live_span, score_span, low)
    score_new = (dot_last(ql, new_latent[0]) + dot_last(qr, new_rope[0])) * scale
    count = new_latent.shape[1]
    row = lax.broadcasted_iota(jnp.int32, (rows, count), 0)
    live_new = column(count) <= lax.rem(row, each) // heads
    score_new = jnp.where(live_new, score_new, low)
    peak = jnp.max(score_mine, axis=1, keepdims=True)
    for other in (score_other, score_span, score_new):
        peak = jnp.maximum(peak, jnp.max(other, axis=1, keepdims=True))
    total = jnp.zeros((rows, 1), jnp.float32)
    weighted = jnp.zeros((rows, width), jnp.float32)
    for score, live, keys in (
        (score_mine, live_mine, mine_latent[0]),
        (score_other, live_other, other_latent[0]),
        (score_span, live_span, span_latent[...]),
        (score_new, live_new, new_latent[0]),
    ):
        weight = jnp.where(live, jnp.exp(score - peak), 0.0)
        total = total + jnp.sum(weight, axis=1, keepdims=True)
        weighted = weighted + dot(weight.astype(jnp.bfloat16), keys)
    out_ref[...] = (weighted / total).astype(jnp.bfloat16).reshape(shards, each, width)


def attention(info, ql, qr, mine, other, span, new, scale, heads, steps):
    shards, stacked, width = ql.shape
    requests, rows, rope_width = qr.shape
    each = stacked // requests
    page_rows = mine[0].shape[1]

    def whole(a):
        return pl.BlockSpec(a.shape, lambda j, info: (0,) * a.ndim)

    def one(a):
        return pl.BlockSpec((1,) + a.shape[1:], lambda j, info: (j, 0, 0))

    by_request = pl.BlockSpec((shards, each, width), lambda j, info: (0, j, 0))
    return pl.pallas_call(
        functools.partial(attention_kernel, scale, heads, page_rows, steps),
        out_shape=jax.ShapeDtypeStruct(ql.shape, jnp.bfloat16),
        grid_spec=pltpu.PrefetchScalarGridSpec(
            num_scalar_prefetch=1,
            grid=(requests,),
            in_specs=[
                by_request,
                one(qr),
                one(mine[0]),
                one(mine[1]),
                one(other[0]),
                one(other[1]),
                whole(span[0]),
                whole(span[1]),
                one(new[0]),
                one(new[1]),
            ],
            out_specs=by_request,
        ),
        compiler_params=pltpu.CompilerParams(vmem_limit_bytes=40 * 1024 * 1024),
    )(info, ql, qr, *mine, *other, *span, *new)


def body(
    states,
    w_latent,
    w_rope,
    latent_gain,
    span_len,
    cache_len,
    dest,
    page_table,
    latent_pool,
    rope_pool,
    new_keys,
    q_nope,
    q_rope,
    w_uk,
    w_uv,
):
    role = lax.axis_index("role")
    roles = lax.axis_size("role")
    own = lax.axis_index("shard")
    shards = lax.axis_size("shard")
    swap = [(0, 1), (1, 0)]
    tok_rows = states.shape[0]
    depth, lat_width = w_latent.shape
    rope_width = w_rope.shape[1]
    requests_each = dest.shape[1]
    request_count = shards * requests_each
    page_rows = latent_pool.shape[1]
    slot_cap = new_keys.shape[1]
    steps = new_keys.shape[2]
    heads_local, head_width, _ = w_uk.shape
    value_width = w_uv.shape[2]
    pages_each = latent_pool.shape[0] // slot_cap
    heads = heads_local // roles
    assert roles == 2 and pages_each * page_rows - tok_rows // 2 == roles * page_rows
    bf16 = jnp.bfloat16

    nope = lax.dynamic_slice_in_dim(q_nope, role * heads * head_width, heads * head_width, axis=2)
    uk = lax.dynamic_slice_in_dim(w_uk, role * heads, heads, axis=0)
    latent_query = jnp.einsum(
        "trhd,hdl->rthl",
        nope.reshape(steps, request_count, heads, head_width),
        uk,
        preferred_element_type=jnp.float32,
    ).astype(bf16)
    latent_query = latent_query.reshape(shards, requests_each * steps * heads, lat_width)
    rotary = lax.dynamic_slice_in_dim(q_rope, role * heads * rope_width, heads * rope_width, axis=2)
    rotary = jnp.swapaxes(rotary, 0, 1).reshape(shards, requests_each * steps, heads * rope_width)

    dest_flat = dest.reshape(-1)
    rank_ids = jnp.arange(shards, dtype=jnp.int32)
    rank_hit = (dest_flat[:, None] == rank_ids[None, :]).astype(jnp.int32)
    slot_of = jnp.sum((jnp.cumsum(rank_hit, axis=0) - rank_hit) * rank_hit, axis=1)
    sender_hit = dest == own
    slot_for = jnp.sum(jnp.where(sender_hit, slot_of.reshape(dest.shape), 0), axis=1)
    page_for = page_table[0][slot_for * pages_each + role]
    latent_cells = jnp.take(latent_pool, page_for, axis=0)
    rope_cells = jnp.take(rope_pool, page_for, axis=0)
    recent = jnp.take(new_keys[0], slot_for, axis=0)
    recent_latent = recent[:, :, :lat_width]
    recent_rope = recent[:, :, lat_width:].reshape(shards, 1, steps * rope_width)
    recent_rope = jnp.pad(
        recent_rope, ((0, 0), (0, 16 - steps - 1), (0, lat_width - steps * rope_width))
    )
    latent_cells = jnp.concatenate([latent_cells, recent_latent, recent_rope], axis=1)

    own_states = lax.dynamic_slice_in_dim(states, role * depth, depth, axis=1)
    partial = jnp.concatenate(
        [
            jnp.dot(own_states, w_latent, preferred_element_type=jnp.float32),
            jnp.dot(own_states, w_rope, preferred_element_type=jnp.float32),
        ],
        axis=1,
    )
    raw = partial + lax.ppermute(partial, "role", swap)
    latent_raw, rope_raw = raw[:, :lat_width], raw[:, lat_width:]
    mean_square = jnp.mean(latent_raw * latent_raw, axis=1, keepdims=True)
    latent_rows = (
        latent_raw * lax.rsqrt(mean_square + 1e-06) * latent_gain.astype(jnp.float32)
    ).astype(bf16)
    own_span, own_cached, own_dest = span_len[own], cache_len[own], dest[own]
    positions = span_positions(own_span, own_cached, tok_rows)
    rope_rows = rotate_rows(rope_raw, positions).astype(bf16)

    got_latent, got_rope, got_query, got_rotary = exchange(
        [latent_cells, rope_cells, latent_query, rotary], shards, 0
    )

    chosen = jnp.take(got_latent, own_dest, axis=0)
    mine = (chosen[:, :page_rows], jnp.take(got_rope, own_dest, axis=0))
    other = tuple(lax.ppermute(a, "role", swap) for a in mine)
    new_latent = chosen[:, page_rows:]
    new_rope = chosen[:, page_rows + steps, : steps * rope_width]
    new_rope = new_rope.reshape(requests_each, steps, rope_width)
    new_rope = jnp.pad(new_rope, ((0, 0), (0, 16 - steps), (0, 0)))
    qr = got_rotary.reshape(shards, requests_each, steps, heads, rope_width)
    qr = jnp.swapaxes(qr, 0, 1).reshape(requests_each, shards * steps * heads, rope_width)
    starts = jnp.cumsum(own_span) - own_span
    info = jnp.concatenate(
        [role[None], jnp.stack([own_cached, starts, own_span], axis=1).reshape(-1)]
    ).astype(jnp.int32)
    attended = attention(
        info,
        got_query,
        qr,
        mine,
        other,
        (latent_rows, rope_rows),
        (new_latent, new_rope),
        (head_width + rope_width) ** (-0.5),
        heads,
        steps,
    )
    (back,) = exchange([attended], shards, 1)
    back = back.reshape(request_count, steps, heads, lat_width)
    uv = lax.dynamic_slice_in_dim(w_uv, role * heads, heads, axis=0)
    projected = jnp.einsum("rthl,hlv->rthv", back, uv, preferred_element_type=jnp.float32)
    projected = projected.astype(bf16).reshape(request_count, steps, heads * value_width)
    half = request_count // roles
    keep = lax.dynamic_slice_in_dim(projected, role * half, half, axis=0)
    give = lax.dynamic_slice_in_dim(projected, (1 - role) * half, half, axis=0)
    got = lax.ppermute(give, "role", swap)
    return jnp.where(
        role == 0,
        jnp.concatenate([keep, got], axis=2),
        jnp.concatenate([got, keep], axis=2),
    )


def solution(mesh):
    return jax.shard_map(
        body,
        mesh=mesh,
        in_specs=(
            P(("parts", "shard"), None),
            P("role", None),
            P("role", None),
            P(),
            P("parts", None),
            P("parts", None),
            P("parts", None),
            P(("parts", "shard"), None),
            P(("parts", "shard"), None, None),
            P(("parts", "shard"), None, None),
            P(("parts", "shard"), None, None, None),
            P(None, "parts", "shard"),
            P(None, "parts", "shard"),
            P("shard", None, None),
            P("shard", None, None),
        ),
        out_specs=P(("parts", "role"), None, "shard"),
        check_vma=False,
    )
```

```python
import functools

import jax
import jax.numpy as jnp
from jax import lax
from jax.experimental import pallas as pl
from jax.experimental.pallas import tpu as pltpu
from jax.sharding import PartitionSpec as P

MESH = pl.DeviceIdType.MESH
CHUNK = 512
LOW = -1e30
LAST = (((1,), (1,)), ((), ()))


def dot(a, b):
    return jnp.dot(a, b, preferred_element_type=jnp.float32)


def dot_last(a, b):
    return lax.dot_general(a, b, LAST, preferred_element_type=jnp.float32)


def iota(shape, axis):
    return lax.broadcasted_iota(jnp.int32, shape, axis)


def one_hot(hit):
    return jnp.where(hit, 1.0, 0.0).astype(jnp.bfloat16)


def kernel(
    dims,
    dest_ref,
    cache_ref,
    span_ref,
    table_ref,
    gain_ref,
    frequency_ref,
    states_hbm,
    w_latent_hbm,
    w_rope_hbm,
    pool_hbm,
    rope_pool_hbm,
    new_latent_hbm,
    new_rope_hbm,
    nope_hbm,
    rotary_hbm,
    uk_hbm,
    uv_hbm,
    out_ref,
    states,
    w_latent,
    w_rope,
    pool,
    rope_pool,
    new_latent,
    new_rope,
    nope,
    uk,
    uv,
    slots,
    k_send,
    k_got,
    r_send,
    r_got,
    q_send,
    q_got,
    rotary_got,
    rotary_rows,
    part_latent,
    part_rope,
    there_latent,
    there_rope,
    span_latent,
    span_rope,
    mine_latent,
    mine_rope,
    other_latent,
    other_rope,
    attended,
    back,
    give,
    taken,
    load_sem,
    k_sem,
    r_sem,
    q_sem,
    rot_sem,
    part_sem,
    page_sem,
    back_sem,
    give_sem,
):
    shards, requests, steps, heads, scale, pages_each = dims
    role = lax.axis_index("role")
    me = lax.axis_index("shard")
    bf16 = jnp.bfloat16
    page_rows, width = pool.shape[1:]
    rope_width = w_rope.shape[1]
    depth = w_latent.shape[0]
    head_width = uk.shape[0] // heads
    value_width = uv.shape[2]
    tokens = states.shape[0]
    each = steps * heads
    query_rows = requests * each
    half = shards // 2
    pair_rows = requests * steps

    loads = [
        (pool_hbm, pool),
        (rope_pool_hbm, rope_pool),
        (new_latent_hbm, new_latent),
        (new_rope_hbm, new_rope),
        (nope_hbm.at[:, pl.ds(pl.multiple_of(role * nope.shape[1], 128), nope.shape[1])], nope),
        (uk_hbm.at[pl.ds(pl.multiple_of(role * uk.shape[0], 128), uk.shape[0])], uk),
        (states_hbm.at[:, pl.ds(pl.multiple_of(role * depth, 128), depth)], states),
        (w_latent_hbm, w_latent),
        (w_rope_hbm, w_rope),
        (uv_hbm.at[pl.ds(role * heads, heads)], uv),
        (
            rotary_hbm.at[
                me, :, pl.ds(pl.multiple_of(role * rotary_got.shape[2], 128), rotary_got.shape[2])
            ],
            rotary_got.at[me],
        ),
    ]
    loads = [pltpu.make_async_copy(a, b, load_sem.at[i]) for i, (a, b) in enumerate(loads)]
    for load in loads:
        load.start()

    barrier = pltpu.get_barrier_semaphore()
    for step in range(1, shards):
        peer = lax.rem(me + step, shards)
        pl.semaphore_signal(barrier, inc=1, device_id={"shard": peer}, device_id_type=MESH)
    pl.semaphore_signal(barrier, inc=1, device_id={"role": 1 - role}, device_id_type=MESH)

    def to_shard(source, target, sem, step, peer):
        return pltpu.make_async_remote_copy(
            src_ref=source,
            dst_ref=target,
            send_sem=sem.at[(0,) + step],
            recv_sem=sem.at[(1,) + step],
            device_id={"shard": peer},
            device_id_type=MESH,
        )

    def to_role(source, target, sem, step):
        return pltpu.make_async_remote_copy(
            src_ref=source,
            dst_ref=target,
            send_sem=sem.at[0, step],
            recv_sem=sem.at[1, step],
            device_id={"role": 1 - role},
            device_id_type=MESH,
        )

    def find(p, count):
        slot = jnp.int32(0)
        for j in range(requests):
            hit = dest_ref[p, j] == me
            slot = jnp.where(hit, count, slot)
            count = count + jnp.where(hit, 1, 0)
        slots[p] = jnp.minimum(slot, new_latent.shape[0] - 1)
        return count

    lax.fori_loop(0, shards, find, jnp.int32(0))
    for load in loads[:4]:
        load.wait()
    pl.semaphore_wait(barrier, shards)

    def k_copy(step, peer, slot):
        return to_shard(k_send.at[peer], k_got.at[slot], k_sem, (step,), peer)

    def r_copy(step, peer, slot):
        return to_shard(r_send.at[peer], r_got.at[slot], r_sem, (step,), peer)

    def q_copy(step, peer, slot):
        return to_shard(q_send.at[peer], q_got.at[slot], q_sem, (step,), peer)

    def rot_copy(step, peer, slot):
        lanes = rotary_got.shape[2]
        source = rotary_hbm.at[peer, :, pl.ds(pl.multiple_of(role * lanes, 128), lanes)]
        return to_shard(source, rotary_got.at[slot], rot_sem, (step,), peer)

    def fill_pages(latent_to, rope_to, peer):
        slot = slots[peer]
        page = table_ref[0, slot * pages_each + role]
        latent_to[:page_rows] = pool[page]
        latent_to[page_rows:] = new_latent[slot]
        rope_to[:rope_width] = rope_pool[page]
        rope_to[rope_width:] = new_rope[slot]

    def send_pages(step, carry):
        peer = lax.rem(me + step, shards)
        fill_pages(k_send.at[peer], r_send.at[peer], peer)
        k_copy(step, peer, me).start()
        r_copy(step, peer, me).start()
        return carry

    lax.fori_loop(1, shards, send_pages, 0)
    for load in loads[4:6]:
        load.wait()

    spread = one_hot(
        lax.div(iota((query_rows, pair_rows), 0), heads) == iota((query_rows, pair_rows), 1)
    )
    shape = (query_rows, heads * head_width)
    own_lanes = lax.div(iota(shape, 1), head_width) == lax.rem(iota(shape, 0), heads)

    def absorb(peer):
        rows = nope[pl.ds(pl.multiple_of(peer * pair_rows, 16), pair_rows), :]
        wide = jnp.where(own_lanes, dot(spread, rows), 0.0).astype(bf16)
        return dot(wide, uk[...]).astype(bf16).reshape(requests, each, width)

    def send_queries(step, carry):
        peer = lax.rem(me + step, shards)
        q_send[peer] = absorb(peer)
        q_copy(step, peer, me).start()
        rot_copy(step, peer, me).start()
        return carry

    lax.fori_loop(1, shards, send_queries, 0)
    q_got[me] = absorb(me)
    fill_pages(k_got.at[me], r_got.at[me], me)

    for load in loads[6:9]:
        load.wait()
    part_latent[...] = jnp.zeros_like(part_latent)
    part_rope[...] = jnp.zeros_like(part_rope)

    def project(k, carry):
        where = pl.ds(pl.multiple_of(k * CHUNK, CHUNK), CHUNK)
        rows = states[:, where]
        part_latent[...] += dot(rows, w_latent[where, :])
        part_rope[...] += dot(rows, w_rope[where, :])
        return carry

    lax.fori_loop(0, depth // CHUNK, project, 0)
    parts = [
        to_role(part_latent, there_latent, part_sem, 0),
        to_role(part_rope, there_rope, part_sem, 1),
    ]
    for copy in parts:
        copy.start()
    position = iota((tokens, 1), 0)
    row = position
    ends = jnp.int32(0)
    for j in range(requests):
        begin = ends
        ends = ends + span_ref[me, j]
        inside = (row >= begin) & (row < ends)
        position = position + jnp.where(inside, cache_ref[me, j] - begin, 0)
    angle = position.astype(jnp.float32) * frequency_ref[...]
    first = iota((tokens, rope_width), 1) < rope_width // 2
    cosine = jnp.cos(angle)
    sine = jnp.sin(angle)
    sine = jnp.where(first, -sine, sine)
    for copy in parts:
        copy.wait()
    raw = part_latent[...] + there_latent[...]
    mean_square = jnp.sum(raw * raw, axis=1, keepdims=True) * (1.0 / width)
    span_latent[...] = (
        raw * lax.rsqrt(mean_square + 1e-06) * gain_ref[...].astype(jnp.float32)
    ).astype(bf16)
    raw = part_rope[...] + there_rope[...]
    turned = jnp.concatenate([raw[:, rope_width // 2 :], raw[:, : rope_width // 2]], axis=1)
    span_rope[...] = (raw * cosine + turned * sine).astype(bf16)

    def take_pages(step, carry):
        origin = lax.rem(me + shards - step, shards)
        k_copy(step, origin, origin).wait_recv()
        r_copy(step, origin, origin).wait_recv()
        return carry

    lax.fori_loop(1, shards, take_pages, 0)
    page_copies = []
    for j in range(requests):
        mine_latent[j] = k_got[dest_ref[me, j]]
        mine_rope[j] = r_got[dest_ref[me, j]]
    for j in range(requests):
        page_copies.append(
            to_role(mine_latent.at[j, pl.ds(0, page_rows)], other_latent.at[j], page_sem, 2 * j)
        )
        page_copies.append(
            to_role(mine_rope.at[j, pl.ds(0, rope_width)], other_rope.at[j], page_sem, 2 * j + 1)
        )
    for copy in page_copies:
        copy.start()

    loads[10].wait()
    lanes = heads * rope_width
    own_rope = lax.div(iota((query_rows, lanes), 1), rope_width) == lax.rem(
        iota((query_rows, lanes), 0), heads
    )
    fold = one_hot(
        lax.rem(iota((lanes, rope_width), 0), rope_width) == iota((lanes, rope_width), 1)
    )

    def unfold(origin):
        wide = jnp.where(own_rope, dot(spread, rotary_got[origin]), 0.0).astype(bf16)
        rotary_rows[origin] = dot(wide, fold).astype(bf16).reshape(requests, each, rope_width)

    unfold(me)

    def take_queries(step, carry):
        origin = lax.rem(me + shards - step, shards)
        rot_copy(step, origin, origin).wait_recv()
        unfold(origin)
        q_copy(step, origin, origin).wait_recv()
        return carry

    lax.fori_loop(1, shards, take_queries, 0)
    for copy in page_copies:
        copy.wait()

    rows = shards * each

    def back_copy(j, step, peer, slot):
        return to_shard(attended.at[j, peer], back.at[slot, j], back_sem, (j, step), peer)

    def attend(j, carry):
        begin = jnp.int32(0)
        for i in range(requests):
            begin = begin + jnp.where(i < j, span_ref[me, i], 0)
        end = begin + span_ref[me, j]
        cached = cache_ref[me, j]
        ql = q_got[:, j].reshape(rows, width)
        qr = rotary_rows[:, j].reshape(rows, rope_width)
        mine = mine_latent[j, :page_rows]
        fresh = mine_latent[j, page_rows:]
        fresh_rope = mine_rope[j, rope_width:, :rope_width]
        other = other_latent[j]
        page_column = iota((rows, page_rows), 1)
        span_column = iota((rows, tokens), 1)
        count = fresh.shape[0]
        time = lax.div(lax.rem(iota((rows, count), 0), each), heads)
        groups = (
            (
                dot_last(ql, mine) + dot(qr, mine_rope[j, :rope_width]),
                page_column + role * page_rows < cached,
                mine,
            ),
            (
                dot_last(ql, other) + dot(qr, other_rope[j]),
                page_column + (1 - role) * page_rows < cached,
                other,
            ),
            (
                dot_last(ql, span_latent[...]) + dot_last(qr, span_rope[...]),
                (span_column >= begin) & (span_column < end),
                span_latent[...],
            ),
            (
                dot_last(ql, fresh) + dot_last(qr, fresh_rope),
                iota((rows, count), 1) <= time,
                fresh,
            ),
        )
        scores = [jnp.where(live, score * scale, LOW) for score, live, _ in groups]
        peak = jnp.max(scores[0], axis=1, keepdims=True)
        for score in scores[1:]:
            peak = jnp.maximum(peak, jnp.max(score, axis=1, keepdims=True))
        total = jnp.zeros((rows, 1), jnp.float32)
        weighted = jnp.zeros((rows, width), jnp.float32)
        for score, (_, live, keys) in zip(scores, groups):
            weight = jnp.where(live, jnp.exp(score - peak), 0.0)
            total = total + jnp.sum(weight, axis=1, keepdims=True)
            weighted = weighted + dot(weight.astype(bf16), keys)
        attended[j] = (weighted / total).astype(bf16).reshape(shards, each, width)

        def send(step, inner):
            peer = lax.rem(me + step, shards)
            back_copy(j, step, peer, me).start()
            return inner

        lax.fori_loop(1, shards, send, 0)
        back[me, j] = attended[j, me]
        return carry

    lax.fori_loop(0, requests, attend, 0)
    loads[9].wait()

    def arrived(p):
        step = lax.rem(me - p + shards, shards)

        @pl.when(step > 0)
        def _():
            for j in range(requests):
                back_copy(j, step, p, p).wait_recv()

    def values(p, h):
        own = back[p].reshape(query_rows, width)
        pick = one_hot(
            iota((pair_rows, query_rows), 1) == iota((pair_rows, query_rows), 0) * heads + h
        )
        return dot(pick, dot(own, uv[h]).astype(bf16)).astype(bf16)

    def give_copy(i):
        return to_role(give.at[i], taken.at[i], give_sem, i)

    def give_rows(i, carry):
        p = (1 - role) * half + i
        arrived(p)
        for h in range(heads):
            give[i, :, h * value_width : (h + 1) * value_width] = values(p, h)
        give_copy(i).start()
        return carry

    lax.fori_loop(0, half, give_rows, 0)
    out_lanes = heads * value_width

    def keep_rows(i, carry):
        p = role * half + i
        arrived(p)
        for h in range(heads):
            lane = pl.multiple_of(role * out_lanes + h * value_width, 128)
            out_ref[pl.ds(pl.multiple_of(i * pair_rows, 16), pair_rows), pl.ds(lane, value_width)] = (
                values(p, h)
            )
        return carry

    lax.fori_loop(0, half, keep_rows, 0)

    def place(i, carry):
        give_copy(i).wait()
        lane = pl.multiple_of((1 - role) * out_lanes, 128)
        out_ref[pl.ds(pl.multiple_of(i * pair_rows, 16), pair_rows), pl.ds(lane, out_lanes)] = taken[i]
        return carry

    lax.fori_loop(0, half, place, 0)

    def drain(step, carry):
        peer = lax.rem(me + step, shards)
        k_copy(step, peer, me).wait_send()
        r_copy(step, peer, me).wait_send()
        q_copy(step, peer, me).wait_send()
        rot_copy(step, peer, me).wait_send()
        for j in range(requests):
            back_copy(j, step, peer, me).wait_send()
        return carry

    lax.fori_loop(1, shards, drain, 0)


def body(
    states,
    w_latent,
    w_rope,
    latent_gain,
    span_len,
    cache_len,
    dest,
    page_table,
    latent_pool,
    rope_pool,
    new_keys,
    q_nope,
    q_rope,
    w_uk,
    w_uv,
):
    roles = lax.axis_size("role")
    shards = lax.axis_size("shard")
    tokens = states.shape[0]
    depth, width = w_latent.shape
    rope_width = w_rope.shape[1]
    requests = dest.shape[1]
    request_count = shards * requests
    pages, page_rows, _ = latent_pool.shape
    slot_cap, steps = new_keys.shape[1:3]
    heads_local, head_width, _ = w_uk.shape
    value_width = w_uv.shape[2]
    pages_each = pages // slot_cap
    heads = heads_local // roles
    assert roles == 2 and pages_each * page_rows - tokens // 2 == roles * page_rows
    each = steps * heads
    pair_rows = requests * steps
    half = shards // 2
    bf16, f32 = jnp.bfloat16, jnp.float32

    half_width = rope_width // 2
    frequency = 10000.0 ** (-jnp.arange(half_width, dtype=f32) / half_width)
    frequency = jnp.concatenate([frequency, frequency])[None, :]
    nope = jnp.swapaxes(q_nope, 0, 1).reshape(request_count * steps, -1)
    rotary = jnp.swapaxes(q_rope, 0, 1).reshape(shards, pair_rows, -1)
    recent = jnp.pad(new_keys[0], ((0, 0), (0, 16 - steps), (0, 128 - rope_width)))
    new_latent, new_rope = recent[:, :, :width], recent[:, :, width:]

    smem = pl.BlockSpec(memory_space=pltpu.SMEM)
    vmem = pl.BlockSpec(memory_space=pltpu.VMEM)
    anywhere = pl.BlockSpec(memory_space=pl.ANY)
    dims = (
        shards, requests, steps, heads, (head_width + rope_width) ** (-0.5), pages_each
    )
    sem = pltpu.SemaphoreType.DMA
    out = pl.pallas_call(
        functools.partial(kernel, dims),
        out_shape=jax.ShapeDtypeStruct((half * pair_rows, heads_local * value_width), bf16),
        in_specs=[smem] * 4 + [vmem] * 2 + [anywhere] * 11,
        out_specs=vmem,
        scratch_shapes=[
            pltpu.VMEM((tokens, depth), bf16),
            pltpu.VMEM((depth, width), bf16),
            pltpu.VMEM((depth, rope_width), bf16),
            pltpu.VMEM(latent_pool.shape, bf16),
            pltpu.VMEM(rope_pool.shape, bf16),
            pltpu.VMEM(new_latent.shape, bf16),
            pltpu.VMEM(new_rope.shape, bf16),
            pltpu.VMEM((request_count * steps, heads * head_width), bf16),
            pltpu.VMEM((heads * head_width, width), bf16),
            pltpu.VMEM((heads, width, value_width), bf16),
            pltpu.SMEM((shards,), jnp.int32),
            pltpu.VMEM((shards, page_rows + 16, width), bf16),
            pltpu.VMEM((shards, page_rows + 16, width), bf16),
            pltpu.VMEM((shards, rope_width + 16, 128), bf16),
            pltpu.VMEM((shards, rope_width + 16, 128), bf16),
            pltpu.VMEM((shards, requests, each, width), bf16),
            pltpu.VMEM((shards, requests, each, width), bf16),
            pltpu.VMEM((shards, pair_rows, heads * rope_width), bf16),
            pltpu.VMEM((shards, requests, each, rope_width), bf16),
            pltpu.VMEM((tokens, width), f32),
            pltpu.VMEM((tokens, rope_width), f32),
            pltpu.VMEM((tokens, width), f32),
            pltpu.VMEM((tokens, rope_width), f32),
            pltpu.VMEM((tokens, width), bf16),
            pltpu.VMEM((tokens, rope_width), bf16),
            pltpu.VMEM((requests, page_rows + 16, width), bf16),
            pltpu.VMEM((requests, rope_width + 16, 128), bf16),
            pltpu.VMEM((requests, page_rows, width), bf16),
            pltpu.VMEM((requests, rope_width, 128), bf16),
            pltpu.VMEM((requests, shards, each, width), bf16),
            pltpu.VMEM((shards, requests, each, width), bf16),
            pltpu.VMEM((half, pair_rows, heads * value_width), bf16),
            pltpu.VMEM((half, pair_rows, heads * value_width), bf16),
            sem((11,)),
            sem((2, shards)),
            sem((2, shards)),
            sem((2, shards)),
            sem((2, shards)),
            sem((2, 2)),
            sem((2, 2 * requests)),
            sem((2, requests, shards)),
            sem((2, half)),
        ],
        compiler_params=pltpu.CompilerParams(
            collective_id=0, has_side_effects=True, vmem_limit_bytes=56 * 1024 * 1024
        ),
    )(
        dest, cache_len, span_len, page_table, latent_gain[None, :], frequency,
        states, w_latent, w_rope, latent_pool, rope_pool, new_latent, new_rope, nope, rotary,
        w_uk.reshape(heads_local * head_width, width), w_uv,
    )
    return out.reshape(request_count // roles, steps, heads_local * value_width)


def solution(mesh):
    return jax.shard_map(
        body,
        mesh=mesh,
        in_specs=(
            P(("parts", "shard"), None),
            P("role", None),
            P("role", None),
            P(),
            P("parts", None),
            P("parts", None),
            P("parts", None),
            P(("parts", "shard"), None),
            P(("parts", "shard"), None, None),
            P(("parts", "shard"), None, None),
            P(("parts", "shard"), None, None, None),
            P(None, "parts", "shard"),
            P(None, "parts", "shard"),
            P("shard", None, None),
            P("shard", None, None),
        ),
        out_specs=P(("parts", "role"), None, "shard"),
        check_vma=False,
    )
```

```python
import functools
import math

import jax
import jax.numpy as jnp
from jax import lax
from jax.experimental import pallas as pl
from jax.experimental.pallas import tpu as pltpu
from jax.sharding import PartitionSpec as P

MESH = pl.DeviceIdType.MESH
CHUNK = 512
LOW = -1e30
LAST = (((1,), (1,)), ((), ()))


def dot(a, b):
    return jnp.dot(a, b, preferred_element_type=jnp.float32)


def dot_last(a, b):
    return lax.dot_general(a, b, LAST, preferred_element_type=jnp.float32)


def iota(shape, axis):
    return lax.broadcasted_iota(jnp.int32, shape, axis)


def one_hot(hit):
    return jnp.where(hit, 1.0, 0.0).astype(jnp.bfloat16)


def kernel(
    dims,
    dest_ref,
    cache_ref,
    span_ref,
    table_ref,
    gain_ref,
    states_hbm,
    w_latent_hbm,
    w_rope_hbm,
    pool_hbm,
    rope_pool_hbm,
    new_keys_hbm,
    nope_hbm,
    rotary_hbm,
    uk_hbm,
    uv_hbm,
    out_ref,
    states,
    w_latent,
    w_rope,
    pool,
    rope_pool,
    new_keys,
    nope,
    rotary,
    uk,
    uv,
    uv_wide,
    slots,
    k_send,
    k_got,
    r_send,
    r_got,
    q_send,
    q_got,
    rotary_send,
    rotary_got,
    rotary_rows,
    part_latent,
    part_rope,
    there_latent,
    there_rope,
    span_latent,
    span_rope,
    mine_latent,
    mine_rope,
    other_latent,
    other_rope,
    attended,
    back,
    give,
    taken,
    load_sem,
    k_sem,
    r_sem,
    q_sem,
    rot_sem,
    part_sem,
    page_sem,
    back_sem,
    give_sem,
):
    shards, requests, steps, heads, scale, pages_each = dims
    role = lax.axis_index("role")
    me = lax.axis_index("shard")
    bf16 = jnp.bfloat16
    page_rows, width = pool.shape[1:]
    rope_width = w_rope.shape[0]
    depth = w_latent.shape[0]
    head_width = uk.shape[0] // heads
    value_width = uv.shape[2]
    tokens = states.shape[0]
    each = steps * heads
    query_rows = requests * each
    half = shards // 2
    pair_rows = requests * steps

    def own_lanes_of(source, target):
        lanes = target.shape[-1]
        return source.at[:, :, pl.ds(pl.multiple_of(role * lanes, 128), lanes)]

    loads = [
        (pool_hbm, pool),
        (rope_pool_hbm, rope_pool),
        (new_keys_hbm.at[0], new_keys),
        (own_lanes_of(nope_hbm, nope), nope),
        (own_lanes_of(rotary_hbm, rotary), rotary),
        (uk_hbm.at[pl.ds(pl.multiple_of(role * uk.shape[0], 128), uk.shape[0])], uk),
        (states_hbm.at[:, pl.ds(pl.multiple_of(role * depth, 128), depth)], states),
        (w_latent_hbm, w_latent),
        (w_rope_hbm, w_rope),
        (uv_hbm.at[pl.ds(role * heads, heads)], uv),
    ]
    loads = [pltpu.make_async_copy(a, b, load_sem.at[i]) for i, (a, b) in enumerate(loads)]
    for load in loads[:6]:
        load.start()

    barrier = pltpu.get_barrier_semaphore()
    for step in range(1, shards):
        peer = lax.rem(me + step, shards)
        pl.semaphore_signal(barrier, inc=1, device_id={"shard": peer}, device_id_type=MESH)
    pl.semaphore_signal(barrier, inc=1, device_id={"role": 1 - role}, device_id_type=MESH)

    def to_shard(source, target, sem, step, peer):
        return pltpu.make_async_remote_copy(
            src_ref=source,
            dst_ref=target,
            send_sem=sem.at[(0,) + step],
            recv_sem=sem.at[(1,) + step],
            device_id={"shard": peer},
            device_id_type=MESH,
        )

    def to_role(source, target, sem, step):
        return pltpu.make_async_remote_copy(
            src_ref=source,
            dst_ref=target,
            send_sem=sem.at[0, step],
            recv_sem=sem.at[1, step],
            device_id={"role": 1 - role},
            device_id_type=MESH,
        )

    def find(p, count):
        slot = jnp.int32(0)
        for j in range(requests):
            hit = dest_ref[j, p] == me
            slot = jnp.where(hit, count, slot)
            count = count + jnp.where(hit, 1, 0)
        slots[p] = jnp.minimum(slot, new_keys.shape[0] - 1)
        return count

    lax.fori_loop(0, shards, find, jnp.int32(0))
    for load in loads[:3]:
        load.wait()
    pl.semaphore_wait(barrier, shards)

    def k_copy(step, peer, slot):
        return to_shard(k_send.at[peer], k_got.at[slot], k_sem, (step,), peer)

    def r_copy(step, peer, slot):
        return to_shard(r_send.at[peer], r_got.at[slot], r_sem, (step,), peer)

    def q_copy(step, peer, slot):
        return to_shard(q_send.at[peer], q_got.at[slot], q_sem, (step,), peer)

    def rot_copy(step, peer, slot):
        return to_shard(rotary_send.at[peer], rotary_got.at[slot], rot_sem, (step,), peer)

    def fill_pages(latent_to, rope_to, peer):
        slot = slots[peer]
        page = table_ref[0, slot * pages_each + role]
        latent_to[...] = pool[page]
        rope_to[:rope_width] = rope_pool[page]
        recent = new_keys[slot]
        blank = jnp.zeros((steps, 128 - rope_width), bf16)
        pieces = [recent[:, c * 128 : (c + 1) * 128] for c in range(width // 128)]
        pieces.append(jnp.concatenate([recent[:, width:], blank], axis=1))
        pieces.append(jnp.zeros((rope_to.shape[0] - rope_width - steps * len(pieces), 128), bf16))
        rope_to[rope_width:] = jnp.concatenate(pieces, axis=0)

    def send_pages(step, carry):
        peer = lax.rem(me + step, shards)
        fill_pages(k_send.at[peer], r_send.at[peer], peer)
        k_copy(step, peer, me).start()
        r_copy(step, peer, me).start()
        return carry

    lax.fori_loop(1, shards, send_pages, 0)
    for load in loads[3:6]:
        load.wait()
    for load in loads[6:]:
        load.start()

    request_count = shards * requests
    all_rows = steps * request_count
    pair = (pair_rows, all_rows)
    pair_source = lax.rem(iota(pair, 0), steps) * request_count + lax.div(iota(pair, 0), steps)
    spread = one_hot(
        lax.div(iota((query_rows, pair_rows), 0), heads) == iota((query_rows, pair_rows), 1)
    )
    shape = (query_rows, heads * head_width)
    own_lanes = lax.div(iota(shape, 1), head_width) == lax.rem(iota(shape, 0), heads)

    def absorb(peer):
        pick = one_hot(iota(pair, 1) == pair_source + peer * requests)
        rows = dot(pick, nope[...].reshape(all_rows, heads * head_width)).astype(bf16)
        rotary_rows_of = dot(pick, rotary[...].reshape(all_rows, heads * rope_width)).astype(bf16)
        wide = jnp.where(own_lanes, dot(spread, rows), 0.0).astype(bf16)
        return dot(wide, uk[...]).astype(bf16).reshape(requests, each, width), rotary_rows_of

    def send_queries(step, carry):
        peer = lax.rem(me + step, shards)
        q_send[peer], rotary_send[peer] = absorb(peer)
        q_copy(step, peer, me).start()
        rot_copy(step, peer, me).start()
        return carry

    lax.fori_loop(1, shards, send_queries, 0)
    q_got[me], rotary_got[me] = absorb(me)
    fill_pages(k_got.at[me], r_got.at[me], me)

    for load in loads[6:9]:
        load.wait()
    part_latent[...] = jnp.zeros_like(part_latent)
    part_rope[...] = jnp.zeros_like(part_rope)

    def project(k, carry):
        where = pl.ds(pl.multiple_of(k * CHUNK, CHUNK), CHUNK)
        rows = states[:, where]
        part_latent[...] += dot(rows, w_latent[where, :])
        part_rope[...] += dot_last(rows, w_rope[:, where])
        return carry

    lax.fori_loop(0, depth // CHUNK, project, 0)
    parts = [
        to_role(part_latent, there_latent, part_sem, 0),
        to_role(part_rope, there_rope, part_sem, 1),
    ]
    for copy in parts:
        copy.start()
    position = iota((tokens, 1), 0)
    row = position
    ends = jnp.int32(0)
    for j in range(requests):
        begin = ends
        ends = ends + span_ref[j, me]
        inside = (row >= begin) & (row < ends)
        position = position + jnp.where(inside, cache_ref[j, me] - begin, 0)
    rank = lax.rem(iota((1, rope_width), 1), rope_width // 2).astype(jnp.float32)
    frequency = jnp.exp(rank * (-math.log(10000.0) / (rope_width // 2)))
    angle = position.astype(jnp.float32) * frequency
    first = iota((tokens, rope_width), 1) < rope_width // 2
    cosine = jnp.cos(angle)
    sine = jnp.sin(angle)
    sine = jnp.where(first, -sine, sine)
    for copy in parts:
        copy.wait()
    raw = part_latent[...] + there_latent[...]
    mean_square = jnp.sum(raw * raw, axis=1, keepdims=True) * (1.0 / width)
    span_latent[...] = (
        raw * lax.rsqrt(mean_square + 1e-06) * gain_ref[...].astype(jnp.float32).reshape(1, width)
    ).astype(bf16)
    raw = part_rope[...] + there_rope[...]
    turned = jnp.concatenate([raw[:, rope_width // 2 :], raw[:, : rope_width // 2]], axis=1)
    span_rope[...] = (raw * cosine + turned * sine).astype(bf16)

    loads[9].wait()
    for h in range(heads):
        uv_wide[:, h * value_width : (h + 1) * value_width] = uv[h]

    def take_pages(step, carry):
        origin = lax.rem(me + shards - step, shards)
        k_copy(step, origin, origin).wait_recv()
        r_copy(step, origin, origin).wait_recv()
        return carry

    lax.fori_loop(1, shards, take_pages, 0)
    page_copies = []
    for j in range(requests):
        mine_latent[j] = k_got[dest_ref[j, me]]
        mine_rope[j] = r_got[dest_ref[j, me]]
    for j in range(requests):
        page_copies.append(
            to_role(mine_latent.at[j], other_latent.at[j], page_sem, 2 * j)
        )
        page_copies.append(
            to_role(mine_rope.at[j, pl.ds(0, rope_width)], other_rope.at[j], page_sem, 2 * j + 1)
        )
    for copy in page_copies:
        copy.start()

    lanes = heads * rope_width
    own_rope = lax.div(iota((query_rows, lanes), 1), rope_width) == lax.rem(
        iota((query_rows, lanes), 0), heads
    )
    fold = one_hot(
        lax.rem(iota((lanes, rope_width), 0), rope_width) == iota((lanes, rope_width), 1)
    )

    def unfold(origin):
        wide = jnp.where(own_rope, dot(spread, rotary_got[origin]), 0.0).astype(bf16)
        rotary_rows[origin] = dot(wide, fold).astype(bf16).reshape(requests, each, rope_width)

    unfold(me)

    def take_queries(step, carry):
        origin = lax.rem(me + shards - step, shards)
        rot_copy(step, origin, origin).wait_recv()
        unfold(origin)
        q_copy(step, origin, origin).wait_recv()
        return carry

    lax.fori_loop(1, shards, take_queries, 0)
    for copy in page_copies:
        copy.wait()

    rows = shards * each

    def back_copy(j, step, peer, slot):
        return to_shard(attended.at[j, peer], back.at[slot, j], back_sem, (j, step), peer)

    def attend(j, carry):
        begin = jnp.int32(0)
        for i in range(requests):
            begin = begin + jnp.where(i < j, span_ref[i, me], 0)
        end = begin + span_ref[j, me]
        cached = cache_ref[j, me]
        ql = q_got[:, j].reshape(rows, width)
        qr = rotary_rows[:, j].reshape(rows, rope_width)
        mine = mine_latent[j]
        recent = mine_rope[j, rope_width:]
        chunks = width // 128
        fresh = jnp.concatenate([recent[c * steps : (c + 1) * steps] for c in range(chunks)], axis=1)
        fresh = jnp.concatenate([fresh, jnp.zeros((16 - steps, width), bf16)], axis=0)
        fresh_rope = recent[chunks * steps : chunks * steps + steps, :rope_width]
        fresh_rope = jnp.concatenate(
            [fresh_rope, jnp.zeros((16 - steps, rope_width), bf16)], axis=0
        )
        other = other_latent[j]
        page_column = iota((rows, page_rows), 1)
        span_column = iota((rows, tokens), 1)
        count = fresh.shape[0]
        time = lax.div(lax.rem(iota((rows, count), 0), each), heads)
        groups = (
            (
                dot_last(ql, mine) + dot(qr, mine_rope[j, :rope_width]),
                page_column + role * page_rows < cached,
                mine,
            ),
            (
                dot_last(ql, other) + dot(qr, other_rope[j]),
                page_column + (1 - role) * page_rows < cached,
                other,
            ),
            (
                dot_last(ql, span_latent[...]) + dot_last(qr, span_rope[...]),
                (span_column >= begin) & (span_column < end),
                span_latent[...],
            ),
            (
                dot_last(ql, fresh) + dot_last(qr, fresh_rope),
                iota((rows, count), 1) <= time,
                fresh,
            ),
        )
        scores = [jnp.where(live, score * scale, LOW) for score, live, _ in groups]
        peak = jnp.max(scores[0], axis=1, keepdims=True)
        for score in scores[1:]:
            peak = jnp.maximum(peak, jnp.max(score, axis=1, keepdims=True))
        total = jnp.zeros((rows, 1), jnp.float32)
        weighted = jnp.zeros((rows, width), jnp.float32)
        for score, (_, live, keys) in zip(scores, groups):
            weight = jnp.where(live, jnp.exp(score - peak), 0.0)
            total = total + jnp.sum(weight, axis=1, keepdims=True)
            weighted = weighted + dot(weight.astype(bf16), keys)
        attended[j] = (weighted / total).astype(bf16).reshape(shards, each, width)

        def send(step, inner):
            peer = lax.rem(me + step, shards)
            back_copy(j, step, peer, me).start()
            return inner

        lax.fori_loop(1, shards, send, 0)
        back[me, j] = attended[j, me]
        return carry

    lax.fori_loop(0, requests, attend, 0)

    def arrived(p):
        step = lax.rem(me - p + shards, shards)

        @pl.when(step > 0)
        def _():
            for j in range(requests):
                back_copy(j, step, p, p).wait_recv()

    out_lanes = heads * value_width
    wide_shape = (query_rows, out_lanes)
    head_lanes = lax.div(iota(wide_shape, 1), value_width) == lax.rem(iota(wide_shape, 0), heads)
    gather = one_hot(
        lax.div(iota((pair_rows, query_rows), 1), heads) == iota((pair_rows, query_rows), 0)
    )

    def values(p):
        own = back[p].reshape(query_rows, width)
        wide = jnp.where(head_lanes, dot(own, uv_wide[...]), 0.0).astype(bf16)
        return dot(gather, wide).astype(bf16)

    def give_copy(i):
        return to_role(give.at[i], taken.at[i], give_sem, i)

    def give_rows(i, carry):
        p = (1 - role) * half + i
        arrived(p)
        give[i] = values(p)
        give_copy(i).start()
        return carry

    lax.fori_loop(0, half, give_rows, 0)

    def keep_rows(i, carry):
        p = role * half + i
        arrived(p)
        lane = pl.multiple_of(role * out_lanes, 128)
        out_ref[pl.ds(pl.multiple_of(i * pair_rows, 16), pair_rows), pl.ds(lane, out_lanes)] = values(p)
        return carry

    lax.fori_loop(0, half, keep_rows, 0)

    def place(i, carry):
        give_copy(i).wait()
        lane = pl.multiple_of((1 - role) * out_lanes, 128)
        out_ref[pl.ds(pl.multiple_of(i * pair_rows, 16), pair_rows), pl.ds(lane, out_lanes)] = taken[i]
        return carry

    lax.fori_loop(0, half, place, 0)

    def drain(step, carry):
        peer = lax.rem(me + step, shards)
        k_copy(step, peer, me).wait_send()
        r_copy(step, peer, me).wait_send()
        q_copy(step, peer, me).wait_send()
        rot_copy(step, peer, me).wait_send()
        for j in range(requests):
            back_copy(j, step, peer, me).wait_send()
        return carry

    lax.fori_loop(1, shards, drain, 0)


def body(
    states,
    w_latent,
    w_rope,
    latent_gain,
    span_len,
    cache_len,
    dest,
    page_table,
    latent_pool,
    rope_pool,
    new_keys,
    q_nope,
    q_rope,
    w_uk,
    w_uv,
):
    roles = lax.axis_size("role")
    shards = lax.axis_size("shard")
    tokens = states.shape[0]
    depth, width = w_latent.shape
    rope_width = w_rope.shape[1]
    requests = dest.shape[1]
    request_count = shards * requests
    pages, page_rows, _ = latent_pool.shape
    slot_cap, steps = new_keys.shape[1:3]
    heads_local, head_width, _ = w_uk.shape
    value_width = w_uv.shape[2]
    pages_each = pages // slot_cap
    heads = heads_local // roles
    assert roles == 2 and pages_each * page_rows - tokens // 2 == roles * page_rows
    each = steps * heads
    pair_rows = requests * steps
    half = shards // 2
    bf16, f32 = jnp.bfloat16, jnp.float32

    smem = pl.BlockSpec(memory_space=pltpu.SMEM)
    vmem = pl.BlockSpec(memory_space=pltpu.VMEM)
    anywhere = pl.BlockSpec(memory_space=pl.ANY)
    dims = (
        shards, requests, steps, heads, (head_width + rope_width) ** (-0.5), pages_each
    )
    sem = pltpu.SemaphoreType.DMA
    tail = -(-(steps * (width // 128 + 1)) // 16) * 16
    out = pl.pallas_call(
        functools.partial(kernel, dims),
        out_shape=jax.ShapeDtypeStruct((half * pair_rows, heads_local * value_width), bf16),
        in_specs=[smem] * 4 + [vmem] + [anywhere] * 10,
        out_specs=vmem,
        scratch_shapes=[
            pltpu.VMEM((tokens, depth), bf16),
            pltpu.VMEM((depth, width), bf16),
            pltpu.VMEM((rope_width, depth), bf16),
            pltpu.VMEM(latent_pool.shape, bf16),
            pltpu.VMEM(rope_pool.shape, bf16),
            pltpu.VMEM(new_keys.shape[1:], bf16),
            pltpu.VMEM((steps, request_count, heads * head_width), bf16),
            pltpu.VMEM((steps, request_count, heads * rope_width), bf16),
            pltpu.VMEM((heads * head_width, width), bf16),
            pltpu.VMEM((heads, width, value_width), bf16),
            pltpu.VMEM((width, heads * value_width), bf16),
            pltpu.SMEM((shards,), jnp.int32),
            pltpu.VMEM((shards, page_rows, width), bf16),
            pltpu.VMEM((shards, page_rows, width), bf16),
            pltpu.VMEM((shards, rope_width + tail, 128), bf16),
            pltpu.VMEM((shards, rope_width + tail, 128), bf16),
            pltpu.VMEM((shards, requests, each, width), bf16),
            pltpu.VMEM((shards, requests, each, width), bf16),
            pltpu.VMEM((shards, pair_rows, heads * rope_width), bf16),
            pltpu.VMEM((shards, pair_rows, heads * rope_width), bf16),
            pltpu.VMEM((shards, requests, each, rope_width), bf16),
            pltpu.VMEM((tokens, width), f32),
            pltpu.VMEM((tokens, rope_width), f32),
            pltpu.VMEM((tokens, width), f32),
            pltpu.VMEM((tokens, rope_width), f32),
            pltpu.VMEM((tokens, width), bf16),
            pltpu.VMEM((tokens, rope_width), bf16),
            pltpu.VMEM((requests, page_rows, width), bf16),
            pltpu.VMEM((requests, rope_width + tail, 128), bf16),
            pltpu.VMEM((requests, page_rows, width), bf16),
            pltpu.VMEM((requests, rope_width, 128), bf16),
            pltpu.VMEM((requests, shards, each, width), bf16),
            pltpu.VMEM((shards, requests, each, width), bf16),
            pltpu.VMEM((half, pair_rows, heads * value_width), bf16),
            pltpu.VMEM((half, pair_rows, heads * value_width), bf16),
            sem((10,)),
            sem((2, shards)),
            sem((2, shards)),
            sem((2, shards)),
            sem((2, shards)),
            sem((2, 2)),
            sem((2, 2 * requests)),
            sem((2, requests, shards)),
            sem((2, half)),
        ],
        compiler_params=pltpu.CompilerParams(
            collective_id=0, has_side_effects=True, vmem_limit_bytes=56 * 1024 * 1024
        ),
    )(
        dest.T, cache_len.T, span_len.T, page_table, latent_gain,
        states, w_latent, w_rope.T, latent_pool, rope_pool, new_keys, q_nope, q_rope,
        w_uk.reshape(heads_local * head_width, width), w_uv,
    )
    return out.reshape(request_count // roles, steps, heads_local * value_width)


def solution(mesh):
    return jax.shard_map(
        body,
        mesh=mesh,
        in_specs=(
            P(("parts", "shard"), None),
            P("role", None),
            P("role", None),
            P(),
            P("parts", None),
            P("parts", None),
            P("parts", None),
            P(("parts", "shard"), None),
            P(("parts", "shard"), None, None),
            P(("parts", "shard"), None, None),
            P(("parts", "shard"), None, None, None),
            P(None, "parts", "shard"),
            P(None, "parts", "shard"),
            P("shard", None, None),
            P("shard", None, None),
        ),
        out_specs=P(("parts", "role"), None, "shard"),
        check_vma=False,
    )
```

```python
import functools
import math

import jax
import jax.numpy as jnp
from jax import lax
from jax.experimental import pallas as pl
from jax.experimental.pallas import tpu as pltpu
from jax.sharding import PartitionSpec as P

MESH = pl.DeviceIdType.MESH
CHUNK = 512
LOW = -1e30
LAST = (((1,), (1,)), ((), ()))


def dot(a, b):
    return jnp.dot(a, b, preferred_element_type=jnp.float32)


def dot_last(a, b):
    return lax.dot_general(a, b, LAST, preferred_element_type=jnp.float32)


def iota(shape, axis):
    return lax.broadcasted_iota(jnp.int32, shape, axis)


def one_hot(hit):
    return jnp.where(hit, 1.0, 0.0).astype(jnp.bfloat16)


def far_first(shards, act):
    middle = shards // 2

    def pair(k, carry):
        act(middle - k, 0)
        act(middle + k, 0)
        return carry

    act(middle, 0)
    lax.fori_loop(1, middle, pair, 0)


def kernel(
    dims,
    dest_ref,
    cache_ref,
    span_ref,
    table_ref,
    gain_ref,
    states_hbm,
    w_latent_hbm,
    w_rope_hbm,
    pool_hbm,
    rope_pool_hbm,
    new_keys_hbm,
    nope_hbm,
    rotary_hbm,
    uk_hbm,
    uv_hbm,
    out_ref,
    states,
    w_latent,
    w_rope,
    pool,
    rope_pool,
    new_keys,
    nope,
    rotary,
    uk,
    uv,
    uv_wide,
    slots,
    k_send,
    k_got,
    r_send,
    r_got,
    q_send,
    q_got,
    rotary_send,
    rotary_got,
    rotary_rows,
    part_latent,
    part_rope,
    there_latent,
    there_rope,
    span_latent,
    span_rope,
    mine_latent,
    mine_rope,
    other_latent,
    other_rope,
    attended,
    back,
    give,
    taken,
    load_sem,
    k_sem,
    r_sem,
    q_sem,
    rot_sem,
    part_sem,
    page_sem,
    back_sem,
    give_sem,
):
    shards, requests, steps, heads, scale, pages_each = dims
    role = lax.axis_index("role")
    me = lax.axis_index("shard")
    bf16 = jnp.bfloat16
    page_rows, width = pool.shape[1:]
    rope_width = w_rope.shape[0]
    depth = w_latent.shape[0]
    head_width = uk.shape[0] // heads
    value_width = uv.shape[2]
    tokens = states.shape[0]
    each = steps * heads
    query_rows = requests * each
    half = shards // 2
    pair_rows = requests * steps

    def own_lanes_of(source, target):
        lanes = target.shape[-1]
        return source.at[:, :, pl.ds(pl.multiple_of(role * lanes, 128), lanes)]

    loads = [
        (pool_hbm, pool),
        (rope_pool_hbm, rope_pool),
        (new_keys_hbm.at[0], new_keys),
        (own_lanes_of(nope_hbm, nope), nope),
        (own_lanes_of(rotary_hbm, rotary), rotary),
        (uk_hbm.at[pl.ds(pl.multiple_of(role * uk.shape[0], 128), uk.shape[0])], uk),
        (states_hbm.at[:, pl.ds(pl.multiple_of(role * depth, 128), depth)], states),
        (w_latent_hbm, w_latent),
        (w_rope_hbm, w_rope),
        (uv_hbm.at[pl.ds(role * heads, heads)], uv),
    ]
    loads = [pltpu.make_async_copy(a, b, load_sem.at[i]) for i, (a, b) in enumerate(loads)]
    for load in loads[:6]:
        load.start()

    barrier = pltpu.get_barrier_semaphore()
    for step in range(1, shards):
        peer = lax.rem(me + step, shards)
        pl.semaphore_signal(barrier, inc=1, device_id={"shard": peer}, device_id_type=MESH)
    pl.semaphore_signal(barrier, inc=1, device_id={"role": 1 - role}, device_id_type=MESH)

    def to_shard(source, target, sem, step, peer):
        return pltpu.make_async_remote_copy(
            src_ref=source,
            dst_ref=target,
            send_sem=sem.at[(0,) + step],
            recv_sem=sem.at[(1,) + step],
            device_id={"shard": peer},
            device_id_type=MESH,
        )

    def to_role(source, target, sem, step):
        return pltpu.make_async_remote_copy(
            src_ref=source,
            dst_ref=target,
            send_sem=sem.at[0, step],
            recv_sem=sem.at[1, step],
            device_id={"role": 1 - role},
            device_id_type=MESH,
        )

    def find(p, count):
        slot = jnp.int32(0)
        for j in range(requests):
            hit = dest_ref[j, p] == me
            slot = jnp.where(hit, count, slot)
            count = count + jnp.where(hit, 1, 0)
        slots[p] = jnp.minimum(slot, new_keys.shape[0] - 1)
        return count

    lax.fori_loop(0, shards, find, jnp.int32(0))
    for load in loads[:3]:
        load.wait()
    pl.semaphore_wait(barrier, shards)

    def k_copy(step, peer, slot):
        return to_shard(k_send.at[peer], k_got.at[slot], k_sem, (step,), peer)

    def r_copy(step, peer, slot):
        return to_shard(r_send.at[peer], r_got.at[slot], r_sem, (step,), peer)

    def q_copy(step, peer, slot):
        return to_shard(q_send.at[peer], q_got.at[slot], q_sem, (step,), peer)

    def rot_copy(step, peer, slot):
        return to_shard(rotary_send.at[peer], rotary_got.at[slot], rot_sem, (step,), peer)

    def fill_pages(latent_to, rope_to, peer):
        slot = slots[peer]
        page = table_ref[0, slot * pages_each + role]
        latent_to[...] = pool[page]
        rope_to[:rope_width] = rope_pool[page]
        recent = new_keys[slot]
        blank = jnp.zeros((steps, 128 - rope_width), bf16)
        pieces = [recent[:, c * 128 : (c + 1) * 128] for c in range(width // 128)]
        pieces.append(jnp.concatenate([recent[:, width:], blank], axis=1))
        pieces.append(jnp.zeros((rope_to.shape[0] - rope_width - steps * len(pieces), 128), bf16))
        rope_to[rope_width:] = jnp.concatenate(pieces, axis=0)

    def send_pages(step, carry):
        peer = lax.rem(me + step, shards)
        fill_pages(k_send.at[peer], r_send.at[peer], peer)
        k_copy(step, peer, me).start()
        r_copy(step, peer, me).start()
        return carry

    far_first(shards, send_pages)
    for load in loads[3:6]:
        load.wait()
    for load in loads[6:]:
        load.start()

    request_count = shards * requests
    all_rows = steps * request_count
    pair = (pair_rows, all_rows)
    pair_source = lax.rem(iota(pair, 0), steps) * request_count + lax.div(iota(pair, 0), steps)
    spread = one_hot(
        lax.div(iota((query_rows, pair_rows), 0), heads) == iota((query_rows, pair_rows), 1)
    )
    shape = (query_rows, heads * head_width)
    own_lanes = lax.div(iota(shape, 1), head_width) == lax.rem(iota(shape, 0), heads)

    def absorb(peer):
        pick = one_hot(iota(pair, 1) == pair_source + peer * requests)
        rows = dot(pick, nope[...].reshape(all_rows, heads * head_width)).astype(bf16)
        rotary_rows_of = dot(pick, rotary[...].reshape(all_rows, heads * rope_width)).astype(bf16)
        wide = jnp.where(own_lanes, dot(spread, rows), 0.0).astype(bf16)
        return dot(wide, uk[...]).astype(bf16).reshape(requests, each, width), rotary_rows_of

    def send_queries(step, carry):
        peer = lax.rem(me + step, shards)
        q_send[peer], rotary_send[peer] = absorb(peer)
        q_copy(step, peer, me).start()
        rot_copy(step, peer, me).start()
        return carry

    far_first(shards, send_queries)
    q_got[me], rotary_got[me] = absorb(me)
    fill_pages(k_got.at[me], r_got.at[me], me)

    for load in loads[6:9]:
        load.wait()
    part_latent[...] = jnp.zeros_like(part_latent)
    part_rope[...] = jnp.zeros_like(part_rope)

    def project(k, carry):
        where = pl.ds(pl.multiple_of(k * CHUNK, CHUNK), CHUNK)
        rows = states[:, where]
        part_latent[...] += dot(rows, w_latent[where, :])
        part_rope[...] += dot_last(rows, w_rope[:, where])
        return carry

    lax.fori_loop(0, depth // CHUNK, project, 0)
    parts = [
        to_role(part_latent, there_latent, part_sem, 0),
        to_role(part_rope, there_rope, part_sem, 1),
    ]
    for copy in parts:
        copy.start()
    position = iota((tokens, 1), 0)
    row = position
    ends = jnp.int32(0)
    for j in range(requests):
        begin = ends
        ends = ends + span_ref[j, me]
        inside = (row >= begin) & (row < ends)
        position = position + jnp.where(inside, cache_ref[j, me] - begin, 0)
    rank = lax.rem(iota((1, rope_width), 1), rope_width // 2).astype(jnp.float32)
    frequency = jnp.exp(rank * (-math.log(10000.0) / (rope_width // 2)))
    angle = position.astype(jnp.float32) * frequency
    first = iota((tokens, rope_width), 1) < rope_width // 2
    cosine = jnp.cos(angle)
    sine = jnp.sin(angle)
    sine = jnp.where(first, -sine, sine)
    for copy in parts:
        copy.wait()
    raw = part_latent[...] + there_latent[...]
    mean_square = jnp.sum(raw * raw, axis=1, keepdims=True) * (1.0 / width)
    span_latent[...] = (
        raw * lax.rsqrt(mean_square + 1e-06) * gain_ref[...].astype(jnp.float32).reshape(1, width)
    ).astype(bf16)
    raw = part_rope[...] + there_rope[...]
    turned = jnp.concatenate([raw[:, rope_width // 2 :], raw[:, : rope_width // 2]], axis=1)
    span_rope[...] = (raw * cosine + turned * sine).astype(bf16)

    loads[9].wait()
    for h in range(heads):
        uv_wide[:, h * value_width : (h + 1) * value_width] = uv[h]

    def take_pages(step, carry):
        origin = lax.rem(me + shards - step, shards)
        k_copy(step, origin, origin).wait_recv()
        r_copy(step, origin, origin).wait_recv()
        return carry

    lax.fori_loop(1, shards, take_pages, 0)
    page_copies = []
    for j in range(requests):
        mine_latent[j] = k_got[dest_ref[j, me]]
        mine_rope[j] = r_got[dest_ref[j, me]]
    for j in range(requests):
        page_copies.append(
            to_role(mine_latent.at[j], other_latent.at[j], page_sem, 2 * j)
        )
        page_copies.append(
            to_role(mine_rope.at[j, pl.ds(0, rope_width)], other_rope.at[j], page_sem, 2 * j + 1)
        )
    for copy in page_copies:
        copy.start()

    lanes = heads * rope_width
    own_rope = lax.div(iota((query_rows, lanes), 1), rope_width) == lax.rem(
        iota((query_rows, lanes), 0), heads
    )
    fold = one_hot(
        lax.rem(iota((lanes, rope_width), 0), rope_width) == iota((lanes, rope_width), 1)
    )

    def unfold(origin):
        wide = jnp.where(own_rope, dot(spread, rotary_got[origin]), 0.0).astype(bf16)
        rotary_rows[origin] = dot(wide, fold).astype(bf16).reshape(requests, each, rope_width)

    unfold(me)

    def take_queries(step, carry):
        origin = lax.rem(me + shards - step, shards)
        rot_copy(step, origin, origin).wait_recv()
        unfold(origin)
        q_copy(step, origin, origin).wait_recv()
        return carry

    far_first(shards, take_queries)
    for copy in page_copies:
        copy.wait()

    rows = shards * each

    def back_copy(j, step, peer, slot):
        return to_shard(attended.at[j, peer], back.at[slot, j], back_sem, (j, step), peer)

    def attend(j, carry):
        begin = jnp.int32(0)
        for i in range(requests):
            begin = begin + jnp.where(i < j, span_ref[i, me], 0)
        end = begin + span_ref[j, me]
        cached = cache_ref[j, me]
        ql = q_got[:, j].reshape(rows, width)
        qr = rotary_rows[:, j].reshape(rows, rope_width)
        mine = mine_latent[j]
        recent = mine_rope[j, rope_width:]
        chunks = width // 128
        fresh = jnp.concatenate([recent[c * steps : (c + 1) * steps] for c in range(chunks)], axis=1)
        fresh = jnp.concatenate([fresh, jnp.zeros((16 - steps, width), bf16)], axis=0)
        fresh_rope = recent[chunks * steps : chunks * steps + steps, :rope_width]
        fresh_rope = jnp.concatenate(
            [fresh_rope, jnp.zeros((16 - steps, rope_width), bf16)], axis=0
        )
        other = other_latent[j]
        page_column = iota((rows, page_rows), 1)
        span_column = iota((rows, tokens), 1)
        count = fresh.shape[0]
        time = lax.div(lax.rem(iota((rows, count), 0), each), heads)
        groups = (
            (
                dot_last(ql, mine) + dot(qr, mine_rope[j, :rope_width]),
                page_column + role * page_rows < cached,
                mine,
            ),
            (
                dot_last(ql, other) + dot(qr, other_rope[j]),
                page_column + (1 - role) * page_rows < cached,
                other,
            ),
            (
                dot_last(ql, span_latent[...]) + dot_last(qr, span_rope[...]),
                (span_column >= begin) & (span_column < end),
                span_latent[...],
            ),
            (
                dot_last(ql, fresh) + dot_last(qr, fresh_rope),
                iota((rows, count), 1) <= time,
                fresh,
            ),
        )
        scores = [jnp.where(live, score * scale, LOW) for score, live, _ in groups]
        peak = jnp.max(scores[0], axis=1, keepdims=True)
        for score in scores[1:]:
            peak = jnp.maximum(peak, jnp.max(score, axis=1, keepdims=True))
        total = jnp.zeros((rows, 1), jnp.float32)
        weighted = jnp.zeros((rows, width), jnp.float32)
        for score, (_, live, keys) in zip(scores, groups):
            weight = jnp.where(live, jnp.exp(score - peak), 0.0)
            total = total + jnp.sum(weight, axis=1, keepdims=True)
            weighted = weighted + dot(weight.astype(bf16), keys)
        attended[j] = (weighted / total).astype(bf16).reshape(shards, each, width)

        def send(step, inner):
            peer = lax.rem(me + step, shards)
            back_copy(j, step, peer, me).start()
            return inner

        far_first(shards, send)
        back[me, j] = attended[j, me]
        return carry

    lax.fori_loop(0, requests, attend, 0)

    def arrived(p):
        step = lax.rem(me - p + shards, shards)

        @pl.when(step > 0)
        def _():
            for j in range(requests):
                back_copy(j, step, p, p).wait_recv()

    out_lanes = heads * value_width
    wide_shape = (query_rows, out_lanes)
    head_lanes = lax.div(iota(wide_shape, 1), value_width) == lax.rem(iota(wide_shape, 0), heads)
    gather = one_hot(
        lax.div(iota((pair_rows, query_rows), 1), heads) == iota((pair_rows, query_rows), 0)
    )

    def values(p):
        own = back[p].reshape(query_rows, width)
        wide = jnp.where(head_lanes, dot(own, uv_wide[...]), 0.0).astype(bf16)
        return dot(gather, wide).astype(bf16)

    def give_copy(i):
        return to_role(give.at[i], taken.at[i], give_sem, i)

    def give_rows(i, carry):
        p = (1 - role) * half + i
        arrived(p)
        give[i] = values(p)
        give_copy(i).start()
        return carry

    lax.fori_loop(0, half, give_rows, 0)

    def keep_rows(i, carry):
        p = role * half + i
        arrived(p)
        lane = pl.multiple_of(role * out_lanes, 128)
        out_ref[pl.ds(pl.multiple_of(i * pair_rows, 16), pair_rows), pl.ds(lane, out_lanes)] = values(p)
        return carry

    lax.fori_loop(0, half, keep_rows, 0)

    def place(i, carry):
        give_copy(i).wait()
        lane = pl.multiple_of((1 - role) * out_lanes, 128)
        out_ref[pl.ds(pl.multiple_of(i * pair_rows, 16), pair_rows), pl.ds(lane, out_lanes)] = taken[i]
        return carry

    lax.fori_loop(0, half, place, 0)

    def drain(step, carry):
        peer = lax.rem(me + step, shards)
        k_copy(step, peer, me).wait_send()
        r_copy(step, peer, me).wait_send()
        q_copy(step, peer, me).wait_send()
        rot_copy(step, peer, me).wait_send()
        for j in range(requests):
            back_copy(j, step, peer, me).wait_send()
        return carry

    lax.fori_loop(1, shards, drain, 0)


def body(
    states,
    w_latent,
    w_rope,
    latent_gain,
    span_len,
    cache_len,
    dest,
    page_table,
    latent_pool,
    rope_pool,
    new_keys,
    q_nope,
    q_rope,
    w_uk,
    w_uv,
):
    roles = lax.axis_size("role")
    shards = lax.axis_size("shard")
    tokens = states.shape[0]
    depth, width = w_latent.shape
    rope_width = w_rope.shape[1]
    requests = dest.shape[1]
    request_count = shards * requests
    pages, page_rows, _ = latent_pool.shape
    slot_cap, steps = new_keys.shape[1:3]
    heads_local, head_width, _ = w_uk.shape
    value_width = w_uv.shape[2]
    pages_each = pages // slot_cap
    heads = heads_local // roles
    assert roles == 2 and pages_each * page_rows - tokens // 2 == roles * page_rows
    each = steps * heads
    pair_rows = requests * steps
    half = shards // 2
    bf16, f32 = jnp.bfloat16, jnp.float32

    smem = pl.BlockSpec(memory_space=pltpu.SMEM)
    vmem = pl.BlockSpec(memory_space=pltpu.VMEM)
    anywhere = pl.BlockSpec(memory_space=pl.ANY)
    dims = (
        shards, requests, steps, heads, (head_width + rope_width) ** (-0.5), pages_each
    )
    sem = pltpu.SemaphoreType.DMA
    tail = -(-(steps * (width // 128 + 1)) // 16) * 16
    out = pl.pallas_call(
        functools.partial(kernel, dims),
        out_shape=jax.ShapeDtypeStruct((half * pair_rows, heads_local * value_width), bf16),
        in_specs=[smem] * 4 + [vmem] + [anywhere] * 10,
        out_specs=vmem,
        scratch_shapes=[
            pltpu.VMEM((tokens, depth), bf16),
            pltpu.VMEM((depth, width), bf16),
            pltpu.VMEM((rope_width, depth), bf16),
            pltpu.VMEM(latent_pool.shape, bf16),
            pltpu.VMEM(rope_pool.shape, bf16),
            pltpu.VMEM(new_keys.shape[1:], bf16),
            pltpu.VMEM((steps, request_count, heads * head_width), bf16),
            pltpu.VMEM((steps, request_count, heads * rope_width), bf16),
            pltpu.VMEM((heads * head_width, width), bf16),
            pltpu.VMEM((heads, width, value_width), bf16),
            pltpu.VMEM((width, heads * value_width), bf16),
            pltpu.SMEM((shards,), jnp.int32),
            pltpu.VMEM((shards, page_rows, width), bf16),
            pltpu.VMEM((shards, page_rows, width), bf16),
            pltpu.VMEM((shards, rope_width + tail, 128), bf16),
            pltpu.VMEM((shards, rope_width + tail, 128), bf16),
            pltpu.VMEM((shards, requests, each, width), bf16),
            pltpu.VMEM((shards, requests, each, width), bf16),
            pltpu.VMEM((shards, pair_rows, heads * rope_width), bf16),
            pltpu.VMEM((shards, pair_rows, heads * rope_width), bf16),
            pltpu.VMEM((shards, requests, each, rope_width), bf16),
            pltpu.VMEM((tokens, width), f32),
            pltpu.VMEM((tokens, rope_width), f32),
            pltpu.VMEM((tokens, width), f32),
            pltpu.VMEM((tokens, rope_width), f32),
            pltpu.VMEM((tokens, width), bf16),
            pltpu.VMEM((tokens, rope_width), bf16),
            pltpu.VMEM((requests, page_rows, width), bf16),
            pltpu.VMEM((requests, rope_width + tail, 128), bf16),
            pltpu.VMEM((requests, page_rows, width), bf16),
            pltpu.VMEM((requests, rope_width, 128), bf16),
            pltpu.VMEM((requests, shards, each, width), bf16),
            pltpu.VMEM((shards, requests, each, width), bf16),
            pltpu.VMEM((half, pair_rows, heads * value_width), bf16),
            pltpu.VMEM((half, pair_rows, heads * value_width), bf16),
            sem((10,)),
            sem((2, shards)),
            sem((2, shards)),
            sem((2, shards)),
            sem((2, shards)),
            sem((2, 2)),
            sem((2, 2 * requests)),
            sem((2, requests, shards)),
            sem((2, half)),
        ],
        compiler_params=pltpu.CompilerParams(
            collective_id=0, has_side_effects=True, vmem_limit_bytes=56 * 1024 * 1024
        ),
    )(
        dest.T, cache_len.T, span_len.T, page_table, latent_gain,
        states, w_latent, w_rope.T, latent_pool, rope_pool, new_keys, q_nope, q_rope,
        w_uk.reshape(heads_local * head_width, width), w_uv,
    )
    return out.reshape(request_count // roles, steps, heads_local * value_width)


def solution(mesh):
    return jax.shard_map(
        body,
        mesh=mesh,
        in_specs=(
            P(("parts", "shard"), None),
            P("role", None),
            P("role", None),
            P(),
            P("parts", None),
            P("parts", None),
            P("parts", None),
            P(("parts", "shard"), None),
            P(("parts", "shard"), None, None),
            P(("parts", "shard"), None, None),
            P(("parts", "shard"), None, None, None),
            P(None, "parts", "shard"),
            P(None, "parts", "shard"),
            P("shard", None, None),
            P("shard", None, None),
        ),
        out_specs=P(("parts", "role"), None, "shard"),
        check_vma=False,
    )
```
